32 devices in a mesh: blk: 16 (over z, y, core), rows: 2 (over x).
Axes of the slice: x: 2, y: 2, z: 4, core: 2. Of those that a mesh axis runs over, the one named last changes fastest.
Arguments:
- panel: bfloat16 [4, 512, 98304], P(None, 'rows', 'blk'), may hold values from -0.01953125 to 0.01953125
- solved: bfloat16 [98304, 1024], P('blk'), may hold values from -6 to 6
- loads: float32 [4, 512, 1024], P(None, 'rows'), may hold values from -6 to 6
- window: bfloat16 [4, 512, 2048], P(None, 'rows'), may hold values from -0.25 to 0.25
- inverses: bfloat16 [4, 512, 512], P(None, 'rows'), as said below
Outputs:
- unknowns: bfloat16 [4, 512, 1024], P(None, 'rows')
The draws below stay inside these ranges and needn't reach their ends.
Inputs may be any that keep to these rules, and one draw needn't show every extreme that they name: inverses[i] is lower triangular, the inverse of the factor's i-th diagonal block.
All inputs are finite; a program needn't handle non-finite values.
Results may differ from the reference program's by a relative error of at most 0.01.
Values may be sent and summed in bfloat16 or wider, within the bound.
No kernel may reach another device: no remote copies, remote signals or barrier semaphores. Data moves between devices by JAX's collectives and lax.ppermute only.
A program may use at most 128 MiB of HBM per device.

```python
import math
import jax
import jax.numpy as jnp
from jax import lax

BS = 512
NSTEP = 4
RHS = 1024
PREVC = 98304


def draw_inverses(key, part):
    key_diag, key_lower = jax.random.split(key)
    diagonal = jax.random.uniform(key_diag, (NSTEP, BS), jnp.float32, 0.6, 1.4)
    strict_lower = jax.random.normal(key_lower, (NSTEP, BS, BS), jnp.float32) * (0.8 / math.sqrt(BS))
    row_index = jnp.arange(BS)[:, None]
    col_index = jnp.arange(BS)[None, :]
    below_mask = (col_index < row_index).astype(jnp.float32)
    identity = (col_index == row_index).astype(jnp.float32)
    return (strict_lower * below_mask + diagonal[:, :, None] * identity).astype(jnp.bfloat16)


def level_of(rng, extent, pieces, least, largest):
    factor_of, own = 1.0, jax.random.fold_in(rng, 6)
    for position, blocks in pieces:
        steps = jnp.exp(jax.random.uniform(jax.random.fold_in(own, position), (blocks,), jnp.float32, least / len(pieces), largest / len(pieces)))
        factor_of = factor_of * jnp.repeat(steps, extent[position] // blocks).reshape([-1 if axis == position else 1 for axis in range(len(extent))])
    return factor_of


def gaussian(stream_key, dims, spread, most, cuts=(), dtype=jnp.bfloat16):
    factor_of = level_of(stream_key, dims, cuts, -0.22, 0.18) if cuts else 1.0
    values = jax.random.normal(stream_key, dims, jnp.float32) * spread * factor_of
    return jnp.minimum(jnp.maximum(values, -most), most).astype(dtype)


def setup_inputs(seed: int = 0) -> dict:
    streams_of = jax.random.split(jax.random.key(seed), 6)
    panel = gaussian(streams_of[0], (NSTEP, BS, PREVC), PREVC ** -0.5, 0.01953125, ((1, 2), (2, 16)))
    solved = gaussian(streams_of[1], (PREVC, RHS), 1.0, 6.0, ((0, 16),))
    loads = gaussian(streams_of[2], (NSTEP, BS, RHS), 1.0, 6.0, ((1, 2),), jnp.float32)
    window = gaussian(streams_of[3], (NSTEP, BS, NSTEP * BS), BS ** -0.5, 0.25, ((1, 2),))
    inverses = draw_inverses(jax.random.fold_in(streams_of[5], 71), 0)
    return dict(panel=panel, solved=solved, loads=loads, window=window, inverses=inverses)


def reference(panel, solved, loads, window, inverses):
    def accumulate(index, running):
        offset = (index * BS).astype(jnp.int32)
        columns = lax.dynamic_slice_in_dim(panel, offset, BS, 2).astype(jnp.float32)
        known = lax.dynamic_slice_in_dim(solved, offset, BS, 0).astype(jnp.float32)
        return running + jnp.einsum("ksc,cr->ksr", columns, known, precision=lax.Precision.HIGHEST)

    totals = lax.fori_loop(0, PREVC // BS, accumulate, jnp.zeros((NSTEP, BS, RHS), jnp.float32))
    results = []
    for current in range(NSTEP):
        residual = loads[current] - totals[current]
        for earlier in range(current):
            coupling = window[current][:, earlier * BS:(earlier + 1) * BS]
            residual = residual - jnp.dot(coupling, results[earlier], preferred_element_type=jnp.float32)
        residual = residual.astype(jnp.bfloat16)
        results.append(jnp.dot(inverses[current], residual, preferred_element_type=jnp.float32).astype(jnp.bfloat16))
    return jnp.stack(results)
```

```python
import functools

import jax
import jax.numpy as jnp
from jax import lax
from jax.experimental import pallas as pl
from jax.experimental.pallas import tpu as pltpu
from jax.sharding import PartitionSpec as P

BF = jnp.bfloat16
F32 = jnp.float32
GROUPS = ((0, 1), (2, 3))
LANES = 128


def swap(value, axis, size, bit):
    step = 1 << bit
    return lax.ppermute(value, axis, [(i, i ^ step) for i in range(size)])


def pick(flag, when_set, when_clear):
    return jnp.where(flag, when_set, when_clear)


def chain_kernel(steps, side_ref, own_w, far_w, own_r, far_r, *rest):
    first = steps[0]
    if first:
        before, own_out, solved, right = rest
        solved[: before.shape[0], :] = before[...]
    else:
        own_out, solved, right = rest
    half = own_r.shape[1]
    block = 2 * half
    side = side_ref[0]
    near_at = pl.multiple_of(side * half, half)
    far_at = pl.multiple_of((1 - side) * half, half)
    offset = 0
    for place, step in enumerate(steps):
        near = own_r[place].astype(F32)
        far = far_r[place].astype(F32)
        inv = slice(offset, offset + block)
        offset += block
        if step:
            win = slice(offset, offset + step * block)
            offset += step * block
            known = solved[: step * block, :]
            near = near - jnp.dot(own_w[:, win], known, preferred_element_type=F32)
            far = far - jnp.dot(far_w[:, win], known, preferred_element_type=F32)
        right[pl.ds(near_at, half), :] = near.astype(BF)
        right[pl.ds(far_at, half), :] = far.astype(BF)
        both = right[...]
        near = jnp.dot(own_w[:, inv], both, preferred_element_type=F32).astype(BF)
        far = jnp.dot(far_w[:, inv], both, preferred_element_type=F32).astype(BF)
        own_out[place] = near
        solved[pl.ds(step * block + near_at, half), :] = near
        solved[pl.ds(step * block + far_at, half), :] = far


def chain(steps, side, own_w, far_w, own_r, far_r, before):
    half, cols = own_r.shape[1:]
    block = 2 * half
    known = (steps[-1] + 1) * block
    args = [side, own_w, far_w, own_r, far_r] + ([before] if steps[0] else [])
    vmem = pl.BlockSpec(memory_space=pltpu.VMEM)
    return pl.pallas_call(
        functools.partial(chain_kernel, steps),
        in_specs=[pl.BlockSpec(memory_space=pltpu.SMEM)] + [vmem] * (len(args) - 1),
        out_specs=[vmem, vmem],
        out_shape=[
            jax.ShapeDtypeStruct((len(steps), half, cols), BF),
            jax.ShapeDtypeStruct((known, cols), BF),
        ],
        scratch_shapes=[pltpu.VMEM((block, cols), BF)],
        compiler_params=pltpu.CompilerParams(vmem_limit_bytes=40 << 20),
        name="chain",
    )(*args)


def shards(size, panel, solved, loads, window, inverses):
    me = lax.axis_index("blk")
    side = lax.axis_index("rows")
    bits = size.bit_length() - 1
    flags = [(me >> bit) & 1 == 1 for bit in range(bits)]
    step_count, half, _ = panel.shape
    block = inverses.shape[2]
    rhs = solved.shape[1]

    halvings = 0
    cols = rhs
    while halvings < bits and cols % (2 * LANES) == 0:
        cols //= 2
        halvings += 1
    place = sum(((me >> bit) & 1) * (rhs >> (bit + 1)) for bit in range(halvings))

    weights = []
    for steps in GROUPS:
        parts = []
        for step in steps:
            parts.append(inverses[step])
            if step:
                parts.append(window[step][:, : step * block])
        own = jnp.concatenate(parts, axis=1)
        mid = own.shape[1] // 2
        sent = pick(flags[0], own[:, mid:], own[:, :mid])
        here = lax.ppermute(sent, "rows", [(0, 1), (1, 0)])
        there = swap(here, "blk", size, 0)
        far = jnp.concatenate(
            [pick(flags[0], there, here), pick(flags[0], here, there)], axis=1
        )
        weights.append((own, far))

    results = []
    known = None
    for steps, (own_w, far_w) in zip(GROUPS, weights):
        count = len(steps)
        rows = panel[steps[0] : steps[-1] + 1].reshape(count * half, -1)
        part = jnp.dot(rows, solved, preferred_element_type=F32).astype(BF)
        for bit in range(halvings):
            mid = part.shape[1] // 2
            low, high = part[:, :mid], part[:, mid:]
            got = swap(pick(flags[bit], low, high), "blk", size, bit)
            part = (pick(flags[bit], high, low).astype(F32) + got.astype(F32)).astype(BF)
        for bit in range(halvings, bits):
            got = swap(part, "blk", size, bit)
            total = part.astype(F32) + got.astype(F32)
            part = total.astype(BF) if bit + 1 < bits else total
        load = lax.dynamic_slice_in_dim(loads[steps[0] : steps[-1] + 1], place, cols, 2)
        remaining = load - part.reshape(count, half, cols).astype(F32)
        far_r = lax.ppermute(remaining.astype(BF), "rows", [(0, 1), (1, 0)])
        answer, known = chain(
            steps, side[None].astype(jnp.int32), own_w, far_w, remaining, far_r, known
        )
        for bit in reversed(range(halvings)):
            got = swap(answer, "blk", size, bit)
            answer = jnp.concatenate(
                [pick(flags[bit], got, answer), pick(flags[bit], answer, got)], axis=2
            )
        results.append(answer)
    return jnp.concatenate(results, axis=0)


def solution(mesh):
    placed = (
        P(None, "rows", "blk"),
        P("blk", None),
        P(None, "rows", None),
        P(None, "rows", None),
        P(None, "rows", None),
    )
    return jax.shard_map(
        functools.partial(shards, mesh.shape["blk"]),
        mesh=mesh,
        in_specs=placed,
        out_specs=P(None, "rows", None),
        check_vma=False,
    )
```

```python
import functools

import jax
import jax.numpy as jnp
from jax import lax
from jax.experimental import pallas as pl
from jax.experimental.pallas import tpu as pltpu
from jax.sharding import PartitionSpec as P

BF = jnp.bfloat16
F32 = jnp.float32
LANES = 128
MIB = 1 << 20
VMEM = pl.BlockSpec(memory_space=pltpu.VMEM)
SMEM = pl.BlockSpec(memory_space=pltpu.SMEM)
ANY = pl.BlockSpec(memory_space=pl.ANY)


def swap(value, axis, size, mask):
    return lax.ppermute(value, axis, [(i, i ^ mask) for i in range(size)])


def pick(flag, when_set, when_clear):
    return jnp.where(flag, when_set, when_clear)


def cost(flops, moved):
    return pl.CostEstimate(flops=flops, bytes_accessed=moved, transcendentals=0)


def in_hbm(value):
    return pltpu.with_memory_space_constraint(value, pltpu.HBM)


def params(mib):
    return pltpu.CompilerParams(vmem_limit_bytes=mib * MIB)


def halve(value, flag, send, keep):
    mid = send.shape[1]
    low, high = value[:, :mid], value[:, mid:]
    send[...] = jnp.where(flag, low, high).astype(send.dtype)
    keep[...] = jnp.where(flag, high, low).astype(keep.dtype)


def gemm_kernel(first, cuts, flag_ref, panel, solved, after, send, keep, rows, held, acc, sem_p, sem_s):
    del after
    count, half, _ = rows.shape
    start = 0
    copies = []
    for index, cut in enumerate(cuts):
        span = slice(start, start + cut)
        start += cut
        copy_p = pltpu.make_async_copy(panel.at[first : first + count, :, span], rows.at[:, :, span], sem_p.at[index])
        copy_s = pltpu.make_async_copy(solved.at[span], held.at[span], sem_s.at[index])
        copy_p.start()
        copy_s.start()
        copies.append((span, copy_p, copy_s))
    flag = flag_ref[0] == 1
    for index, (span, copy_p, copy_s) in enumerate(copies):
        copy_p.wait()
        copy_s.wait()
        part = jnp.dot(
            rows[:, :, span].reshape(count * half, cuts[index]), held[span, :], preferred_element_type=F32
        )
        if index:
            part = part + acc[...]
        if index + 1 < len(cuts):
            acc[...] = part
        else:
            halve(part, flag, send, keep)


def gemm(flag, panel, solved, steps, after):
    _, half, depth = panel.shape
    rhs = solved.shape[1]
    count = len(steps)
    pieces = next(p for p in (6, 8, 4, 3, 2, 1) if depth % (p * LANES) == 0)
    cuts = (depth // pieces,) * pieces
    rows = count * half
    return pl.pallas_call(
        functools.partial(gemm_kernel, steps[0], cuts),
        in_specs=[SMEM, ANY, ANY, ANY],
        out_specs=[VMEM] * 2,
        out_shape=[
            jax.ShapeDtypeStruct((rows, rhs // 2), BF),
            jax.ShapeDtypeStruct((rows, rhs // 2), BF),
        ],
        scratch_shapes=[
            pltpu.VMEM((count, half, depth), BF),
            pltpu.VMEM((depth, rhs), BF),
            pltpu.VMEM((rows, rhs), F32),
            pltpu.SemaphoreType.DMA((pieces,)),
            pltpu.SemaphoreType.DMA((pieces,)),
        ],
        compiler_params=params(30),
        cost_estimate=cost(1, 1),
        name="gemm",
    )(flag, in_hbm(panel), in_hbm(solved), after)


def split_kernel(at_ref, keep, got, *pieces):
    width = pieces[0].shape[1]
    for index, piece in enumerate(pieces):
        span = pl.ds(pl.multiple_of(at_ref[index] * width, width), width)
        piece[...] = (keep[:, span].astype(F32) + got[:, span].astype(F32)).astype(piece.dtype)


def split(at, keep, got, count):
    rows, cols = keep.shape
    return pl.pallas_call(
        split_kernel,
        in_specs=[SMEM, VMEM, VMEM],
        out_specs=[VMEM] * count,
        out_shape=[jax.ShapeDtypeStruct((rows, cols // count), BF if i else F32) for i in range(count)],
        compiler_params=params(16),
        name="split",
    )(at, keep, got)


def far_units(step_count):
    units = []
    for step in range(step_count):
        if step + 1 < step_count:
            units += [("inverses", step, piece) for piece in range(2)]
        units += [("window", step, piece) for piece in range(2 * step)]
    return units


def pack_kernel(flag_ref, inverses, window, out, sems):
    half = out.shape[1]
    sources = {"inverses": inverses, "window": window}
    units = far_units(inverses.shape[0])
    mid = out.shape[0]
    for core in range(2):

        @pl.when(flag_ref[0] == core)
        def _():
            copies = []
            for index, (name, step, piece) in enumerate(units[core * mid : (core + 1) * mid]):
                span = slice(piece * half, (piece + 1) * half)
                copy = pltpu.make_async_copy(sources[name].at[step, :, span], out.at[index], sems.at[index])
                copy.start()
                copies.append(copy)
            for copy in copies:
                copy.wait()


def pack(flag, inverses, window):
    step_count, half, _ = inverses.shape
    mid = (len(far_units(step_count)) + 1) // 2
    return pl.pallas_call(
        pack_kernel,
        in_specs=[SMEM, ANY, ANY],
        out_specs=VMEM,
        out_shape=jax.ShapeDtypeStruct((mid, half, half), BF),
        scratch_shapes=[pltpu.SemaphoreType.DMA((mid,))],
        compiler_params=params(4),
        cost_estimate=cost(1, 4 * mid * half * half),
        name="pack",
    )(flag, in_hbm(inverses), in_hbm(window))


def unpack_kernel(flag_ref, here, there, out, sems):
    mid = here.shape[0]
    flag = flag_ref[0]
    copies = [
        pltpu.make_async_copy(here, out.at[pl.ds(flag * mid, mid)], sems.at[0]),
        pltpu.make_async_copy(there, out.at[pl.ds((1 - flag) * mid, mid)], sems.at[1]),
    ]
    for copy in copies:
        copy.start()
    for copy in copies:
        copy.wait()


def unpack(flag, here, there):
    mid, half, _ = here.shape
    return pl.pallas_call(
        unpack_kernel,
        in_specs=[SMEM, ANY, ANY],
        out_specs=VMEM,
        out_shape=jax.ShapeDtypeStruct((2 * mid, half, half), BF),
        scratch_shapes=[pltpu.SemaphoreType.DMA((2,))],
        compiler_params=params(4),
        cost_estimate=cost(1, 8 * mid * half * half),
        name="unpack",
    )(flag, here, there)


def chain_kernel(steps, side_ref, inverses, window, far_w, own_r, far_r, *rest):
    first = steps[0]
    own_out, solved, right = rest[-3:]
    if first:
        before = rest[0]
        solved[: before.shape[0], :] = before[...]
    step_count, half, block = inverses.shape
    units = far_units(step_count)
    side = side_ref[0]
    near_at = pl.multiple_of(side * half, half)
    far_at = pl.multiple_of((1 - side) * half, half)
    for place, step in enumerate(steps):
        near = own_r[place].astype(F32)
        far = far_r[place].astype(F32)
        if step:
            known = solved[: step * block, :]
            near = near - jnp.dot(window[step, :, : step * block], known, preferred_element_type=F32)
            for piece in range(2 * step):
                known = solved[piece * half : (piece + 1) * half, :]
                tile = far_w[units.index(("window", step, piece))]
                far = far - jnp.dot(tile, known, preferred_element_type=F32)
        right[pl.ds(near_at, half), :] = near.astype(BF)
        right[pl.ds(far_at, half), :] = far.astype(BF)
        near = jnp.dot(inverses[step], right[...], preferred_element_type=F32).astype(BF)
        own_out[place] = near
        if step + 1 < step_count:
            far = jnp.zeros_like(far)
            for piece in range(2):
                tile = far_w[units.index(("inverses", step, piece))]
                far = far + jnp.dot(tile, right[piece * half : (piece + 1) * half, :], preferred_element_type=F32)
            solved[pl.ds(pl.multiple_of(step * block + near_at, half), half), :] = near
            solved[pl.ds(pl.multiple_of(step * block + far_at, half), half), :] = far.astype(BF)


def chain(steps, side, inverses, window, far_w, own_r, far_r, before, after):
    count, half, cols = own_r.shape
    block = 2 * half
    args = [side, inverses, window, far_w, own_r, far_r] + ([before] if steps[0] else [])
    return pl.pallas_call(
        functools.partial(chain_kernel, steps),
        in_specs=[SMEM] + [VMEM] * (len(args) - 1) + [ANY] * len(after),
        out_specs=[VMEM, VMEM],
        out_shape=[
            jax.ShapeDtypeStruct((count, half, cols), BF),
            jax.ShapeDtypeStruct((min(steps[-1] + 1, inverses.shape[0] - 1) * block, cols), BF),
        ],
        scratch_shapes=[pltpu.VMEM((block, cols), BF)],
        compiler_params=params(20),
        name="chain",
    )(*args, *after)


def anchor_kernel(*refs):
    del refs


def anchor(value, after):
    return pl.pallas_call(
        anchor_kernel,
        in_specs=[ANY] * (1 + len(after)),
        out_specs=ANY,
        out_shape=jax.ShapeDtypeStruct(value.shape, value.dtype),
        input_output_aliases={0: 0},
        compiler_params=params(1),
        cost_estimate=cost(1, 1),
        name="anchor",
    )(value, *after)


def put_kernel(firsts, at_ref, *refs):
    out, sems = refs[-2:]
    pieces = refs[:-2]
    per = len(pieces) // len(firsts)
    copies = []
    for index, piece in enumerate(pieces):
        count, _, cols = piece.shape
        first = firsts[index // per]
        span = pl.ds(pl.multiple_of(at_ref[index % per] * cols, cols), cols)
        copy = pltpu.make_async_copy(piece, out.at[first : first + count, :, span], sems.at[index])
        copy.start()
        copies.append(copy)
    for copy in copies:
        copy.wait()


def put(firsts, shape, at, pieces):
    return pl.pallas_call(
        functools.partial(put_kernel, firsts),
        in_specs=[SMEM] + [VMEM] * len(pieces),
        out_specs=ANY,
        out_shape=jax.ShapeDtypeStruct(shape, BF),
        scratch_shapes=[pltpu.SemaphoreType.DMA((len(pieces),))],
        compiler_params=params(16),
        name="put",
    )(at, *pieces)


def cut_kernel(at_ref, loads, after, *refs):
    del after
    outs, sems = refs[:-1], refs[-1]
    cols = outs[0].shape[2]
    span = pl.ds(pl.multiple_of(at_ref[0] * cols, cols), cols)
    copies = []
    first = 0
    for index, out in enumerate(outs):
        copy = pltpu.make_async_copy(loads.at[first : first + out.shape[0], :, span], out, sems.at[index])
        first += out.shape[0]
        copy.start()
        copies.append(copy)
    for copy in copies:
        copy.wait()


def cut(at, loads, cols, counts, after):
    half = loads.shape[1]
    return pl.pallas_call(
        cut_kernel,
        in_specs=[SMEM, ANY, ANY],
        out_specs=[VMEM] * len(counts),
        out_shape=[jax.ShapeDtypeStruct((count, half, cols), F32) for count in counts],
        scratch_shapes=[pltpu.SemaphoreType.DMA((len(counts),))],
        compiler_params=params(4),
        cost_estimate=cost(1, 1 << 23),
        name="cut",
    )(at, in_hbm(loads), after)


def shards(size, panel, solved, loads, window, inverses):
    me = lax.axis_index("blk")
    side = lax.axis_index("rows").astype(jnp.int32)[None]
    bits = size.bit_length() - 1
    flags = [(me >> bit) & 1 for bit in range(bits)]
    step_count, half, _ = panel.shape
    block = inverses.shape[2]
    rhs = solved.shape[1]

    halvings = 1
    while halvings < bits and (rhs >> halvings) % (2 * LANES) == 0:
        halvings += 1
    inner = halvings - 1
    cols = rhs >> halvings
    blocks = 1 << halvings
    mine = sum(flags[bit] << (inner - bit) for bit in range(halvings))
    reverse = [sum(((mask >> bit) & 1) << (inner - bit) for bit in range(halvings)) for mask in range(blocks)]
    cross = [2 * mask for mask in range(1 << inner)]
    split_at = jnp.stack([(mine ^ reverse[mask]) & ((1 << inner) - 1) for mask in cross]).astype(jnp.int32)
    put_at = jnp.stack([mine ^ reverse[mask] for mask in cross + [mask + 1 for mask in cross]]).astype(jnp.int32)
    core = flags[0].astype(jnp.int32)[None]

    pair = [(0, 1), (1, 0)]
    sent = pack(core, inverses, window)
    here = lax.ppermute(sent, "rows", pair)

    first_count = (step_count + 1) // 2
    steps_a, steps_b = tuple(range(first_count)), tuple(range(first_count, step_count))
    shape = (step_count, half, rhs)
    together = lax.optimization_barrier

    def scatter(send, keep):
        pieces = split(split_at, keep, swap(send, "blk", size, 1), len(cross))
        return pieces[0], [swap(piece, "blk", size, mask) for mask, piece in zip(cross[1:], pieces[1:])], pieces[1]

    def collect(own, got):
        for piece in got:
            own = own + piece.astype(F32)
        part = own.astype(BF)
        for bit in range(halvings, bits - 1):
            part = (part.astype(F32) + swap(part, "blk", size, 1 << bit).astype(F32)).astype(BF)
        return part, swap(part, "blk", size, 1 << (bits - 1))

    def remain(load, part, got):
        return load - (part.astype(F32) + got.astype(F32)).reshape(load.shape)

    def spread(answer):
        return [swap(answer, "blk", size, mask) for mask in cross[1:]]

    def forward(answer, got):
        pieces = [answer] + got
        return pieces + [swap(piece, "blk", size, 1) for piece in pieces]

    send, keep = gemm(core, panel, solved, steps_a, sent)
    own_a, got_a, after = scatter(send, keep)
    send, keep = gemm(core, panel, solved, steps_b, after)
    send, got_a = together((send, got_a))
    own_b, got_b, after = scatter(send, keep)
    load_a, load_b = cut(mine.astype(jnp.int32)[None], loads, cols, (len(steps_a), len(steps_b)), after)
    part_a, half_a = collect(own_a, got_a)
    half_a = anchor(half_a, [after])
    got_b[-1] = anchor(got_b[-1], [half_a])
    part_b, half_b = collect(own_b, got_b)
    left_a = remain(load_a, part_a, half_a)
    far_a = lax.ppermute(left_a.astype(BF), "rows", pair)
    there = swap(here, "blk", size, 1)
    far_w = unpack(core, here, there)
    answer_a, known = chain(steps_a, side, inverses, window, far_w, left_a, far_a, None, [])
    got_a = spread(answer_a)
    left_b = remain(load_b, part_b, anchor(half_b, [known]))
    far_b = lax.ppermute(left_b.astype(BF), "rows", pair)
    answer_b, _ = chain(steps_b, side, inverses, window, far_w, left_b, far_b, known, [got_a[0]])
    got_b = spread(answer_b)
    return put((steps_a[0], steps_b[0]), shape, put_at, forward(answer_a, got_a) + forward(answer_b, got_b))


def solution(mesh):
    placed = (
        P(None, "rows", "blk"),
        P("blk", None),
        P(None, "rows", None),
        P(None, "rows", None),
        P(None, "rows", None),
    )
    return jax.shard_map(
        functools.partial(shards, mesh.shape["blk"]),
        mesh=mesh,
        in_specs=placed,
        out_specs=P(None, "rows", None),
        check_vma=False,
    )
```

```python
import functools

import jax
import jax.numpy as jnp
from jax import lax
from jax.experimental import pallas as pl
from jax.experimental.pallas import tpu as pltpu
from jax.sharding import PartitionSpec as P

BF = jnp.bfloat16
F32 = jnp.float32
LANES = 128
MIB = 1 << 20
VMEM = pl.BlockSpec(memory_space=pltpu.VMEM)
SMEM = pl.BlockSpec(memory_space=pltpu.SMEM)
ANY = pl.BlockSpec(memory_space=pl.ANY)


def swap(value, axis, size, mask):
    return lax.ppermute(value, axis, [(i, i ^ mask) for i in range(size)])


def pick(flag, when_set, when_clear):
    return jnp.where(flag, when_set, when_clear)


def cost(flops, moved):
    return pl.CostEstimate(flops=flops, bytes_accessed=moved, transcendentals=0)


def in_hbm(value):
    return pltpu.with_memory_space_constraint(value, pltpu.HBM)


def params(mib):
    return pltpu.CompilerParams(vmem_limit_bytes=mib * MIB)


def halve(value, flag, send, keep):
    mid = send.shape[1]
    low, high = value[:, :mid], value[:, mid:]
    send[...] = jnp.where(flag, low, high).astype(send.dtype)
    keep[...] = jnp.where(flag, high, low).astype(keep.dtype)


def gemm_kernel(first, cuts, flag_ref, panel, solved, *refs):
    send, keep, rows, held, acc, sem_p, sem_s = refs[-7:]
    count, half, _ = rows.shape
    start = 0
    copies = []
    for index, cut in enumerate(cuts):
        span = slice(start, start + cut)
        start += cut
        copy_p = pltpu.make_async_copy(panel.at[first : first + count, :, span], rows.at[:, :, span], sem_p.at[index])
        copy_s = pltpu.make_async_copy(solved.at[span], held.at[span], sem_s.at[index])
        copy_p.start()
        copy_s.start()
        copies.append((span, copy_p, copy_s))
    flag = flag_ref[0] == 1
    for index, (span, copy_p, copy_s) in enumerate(copies):
        copy_p.wait()
        copy_s.wait()
        part = jnp.dot(
            rows[:, :, span].reshape(count * half, cuts[index]), held[span, :], preferred_element_type=F32
        )
        if index:
            part = part + acc[...]
        if index + 1 < len(cuts):
            acc[...] = part
        else:
            halve(part, flag, send, keep)


def gemm(flag, panel, solved, steps, after):
    _, half, depth = panel.shape
    rhs = solved.shape[1]
    count = len(steps)
    pieces = next(p for p in (6, 8, 4, 3, 2, 1) if depth % (p * LANES) == 0)
    cuts = (depth // pieces,) * pieces
    if cuts[-1] % (2 * LANES) == 0:
        cuts = cuts[:-1] + (cuts[-1] // 2,) * 2
    rows = count * half
    return pl.pallas_call(
        functools.partial(gemm_kernel, steps[0], cuts),
        in_specs=[SMEM, ANY, ANY] + [ANY] * len(after),
        out_specs=[VMEM] * 2,
        out_shape=[
            jax.ShapeDtypeStruct((rows, rhs // 2), BF),
            jax.ShapeDtypeStruct((rows, rhs // 2), BF),
        ],
        scratch_shapes=[
            pltpu.VMEM((count, half, depth), BF),
            pltpu.VMEM((depth, rhs), BF),
            pltpu.VMEM((rows, rhs), F32),
            pltpu.SemaphoreType.DMA((len(cuts),)),
            pltpu.SemaphoreType.DMA((len(cuts),)),
        ],
        compiler_params=params(30),
        cost_estimate=cost(1, 1),
        name="gemm",
    )(flag, in_hbm(panel), in_hbm(solved), *after)


def split_kernel(at_ref, keep, got, *pieces):
    width = pieces[0].shape[1]
    for index, piece in enumerate(pieces):
        span = pl.ds(pl.multiple_of(at_ref[index] * width, width), width)
        piece[...] = (keep[:, span].astype(F32) + got[:, span].astype(F32)).astype(piece.dtype)


def split(at, keep, got, count):
    rows, cols = keep.shape
    return pl.pallas_call(
        split_kernel,
        in_specs=[SMEM, VMEM, VMEM],
        out_specs=[VMEM] * count,
        out_shape=[jax.ShapeDtypeStruct((rows, cols // count), BF if i else F32) for i in range(count)],
        compiler_params=params(16),
        name="split",
    )(at, keep, got)


def far_units(groups):
    units = []
    for steps in groups:
        for step in steps:
            if step != groups[-1][-1]:
                units += [("inverses", step, piece) for piece in range(2)]
            units += [("window", step, piece) for piece in range(2 * steps[0], 2 * step)]
    return units


def pack_kernel(units, flag_ref, inverses, window, after, out, sems):
    del after
    half = out.shape[1]
    sources = {"inverses": inverses, "window": window}
    mid = out.shape[0]
    for core in range(2):

        @pl.when(flag_ref[0] == core)
        def _():
            copies = []
            for index, (name, step, piece) in enumerate(units[core * mid : (core + 1) * mid]):
                span = slice(piece * half, (piece + 1) * half)
                copy = pltpu.make_async_copy(sources[name].at[step, :, span], out.at[index], sems.at[index])
                copy.start()
                copies.append(copy)
            for copy in copies:
                copy.wait()


def pack(units, flag, inverses, window, after):
    half = inverses.shape[1]
    mid = (len(units) + 1) // 2
    return pl.pallas_call(
        functools.partial(pack_kernel, units),
        in_specs=[SMEM, ANY, ANY, ANY],
        out_specs=VMEM,
        out_shape=jax.ShapeDtypeStruct((mid, half, half), BF),
        scratch_shapes=[pltpu.SemaphoreType.DMA((mid,))],
        compiler_params=params(4),
        cost_estimate=cost(1, 4 * mid * half * half),
        name="pack",
    )(flag, in_hbm(inverses), in_hbm(window), after)


def unpack_kernel(flag_ref, here, there, out, sems):
    mid = here.shape[0]
    flag = flag_ref[0]
    copies = [
        pltpu.make_async_copy(here, out.at[pl.ds(flag * mid, mid)], sems.at[0]),
        pltpu.make_async_copy(there, out.at[pl.ds((1 - flag) * mid, mid)], sems.at[1]),
    ]
    for copy in copies:
        copy.start()
    for copy in copies:
        copy.wait()


def unpack(flag, here, there):
    mid, half, _ = here.shape
    return pl.pallas_call(
        unpack_kernel,
        in_specs=[SMEM, ANY, ANY],
        out_specs=VMEM,
        out_shape=jax.ShapeDtypeStruct((2 * mid, half, half), BF),
        scratch_shapes=[pltpu.SemaphoreType.DMA((2,))],
        compiler_params=params(4),
        cost_estimate=cost(1, 8 * mid * half * half),
        name="unpack",
    )(flag, here, there)


def chain_kernel(units, steps, last, side_ref, inverses, window, far_w, own_r, far_r, *refs):
    own_out, solved, right = refs[-3:]
    _, half, block = inverses.shape
    start = steps[0]
    side = side_ref[0]
    near_at = pl.multiple_of(side * half, half)
    far_at = pl.multiple_of((1 - side) * half, half)
    for place, step in enumerate(steps):
        near = own_r[place].astype(F32)
        far = far_r[place].astype(F32)
        if place:
            known = solved[: place * block, :]
            near = near - jnp.dot(window[step, :, start * block : step * block], known, preferred_element_type=F32)
            for piece in range(2 * place):
                known = solved[piece * half : (piece + 1) * half, :]
                tile = far_w[units.index(("window", step, 2 * start + piece))]
                far = far - jnp.dot(tile, known, preferred_element_type=F32)
        right[pl.ds(near_at, half), :] = near.astype(BF)
        right[pl.ds(far_at, half), :] = far.astype(BF)
        near = jnp.dot(inverses[step], right[...], preferred_element_type=F32).astype(BF)
        own_out[place] = near
        if step != last:
            far = jnp.zeros_like(far)
            for piece in range(2):
                tile = far_w[units.index(("inverses", step, piece))]
                far = far + jnp.dot(tile, right[piece * half : (piece + 1) * half, :], preferred_element_type=F32)
            solved[pl.ds(pl.multiple_of(place * block + near_at, half), half), :] = near
            solved[pl.ds(pl.multiple_of(place * block + far_at, half), half), :] = far.astype(BF)


def chain(units, steps, side, inverses, window, far_w, own_r, far_r, after):
    count, half, cols = own_r.shape
    block = 2 * half
    last = inverses.shape[0] - 1
    args = [side, inverses, window, far_w, own_r, far_r]
    return pl.pallas_call(
        functools.partial(chain_kernel, units, steps, last),
        in_specs=[SMEM] + [VMEM] * (len(args) - 1) + [ANY] * len(after),
        out_specs=[VMEM, VMEM],
        out_shape=[
            jax.ShapeDtypeStruct((count, half, cols), BF),
            jax.ShapeDtypeStruct((min(count, last - steps[0]) * block, cols), BF),
        ],
        scratch_shapes=[pltpu.VMEM((block, cols), BF)],
        compiler_params=params(8),
        name="chain",
    )(*args, *after)


def couple_kernel(load, window, known, out):
    count, half, _ = load.shape
    flat = window[-count:, :, : known.shape[0]].reshape(count * half, known.shape[0])
    out[...] = load[...] - jnp.dot(flat, known[...], preferred_element_type=F32).reshape(load.shape)


def couple(load, window, known):
    return pl.pallas_call(
        couple_kernel,
        in_specs=[VMEM] * 3,
        out_specs=VMEM,
        out_shape=jax.ShapeDtypeStruct(load.shape, F32),
        compiler_params=params(8),
        name="couple",
    )(load, window, known)


def anchor_kernel(*refs):
    del refs


def anchor(value, after):
    return pl.pallas_call(
        anchor_kernel,
        in_specs=[ANY] * (1 + len(after)),
        out_specs=ANY,
        out_shape=jax.ShapeDtypeStruct(value.shape, value.dtype),
        input_output_aliases={0: 0},
        compiler_params=params(1),
        cost_estimate=cost(1, 1),
        name="anchor",
    )(value, *after)


def put_kernel(firsts, at_ref, *refs):
    out, sems = refs[-2:]
    pieces = refs[:-2]
    per = len(pieces) // len(firsts)
    copies = []
    for index, piece in enumerate(pieces):
        count, _, cols = piece.shape
        first = firsts[index // per]
        span = pl.ds(pl.multiple_of(at_ref[index % per] * cols, cols), cols)
        copy = pltpu.make_async_copy(piece, out.at[first : first + count, :, span], sems.at[index])
        copy.start()
        copies.append(copy)
    for copy in copies:
        copy.wait()


def put(firsts, shape, at, pieces):
    return pl.pallas_call(
        functools.partial(put_kernel, firsts),
        in_specs=[SMEM] + [VMEM] * len(pieces),
        out_specs=ANY,
        out_shape=jax.ShapeDtypeStruct(shape, BF),
        scratch_shapes=[pltpu.SemaphoreType.DMA((len(pieces),))],
        compiler_params=params(16),
        name="put",
    )(at, *pieces)


def cut_kernel(at_ref, loads, after, *refs):
    del after
    outs, sems = refs[:-1], refs[-1]
    cols = outs[0].shape[2]
    span = pl.ds(pl.multiple_of(at_ref[0] * cols, cols), cols)
    copies = []
    first = 0
    for index, out in enumerate(outs):
        copy = pltpu.make_async_copy(loads.at[first : first + out.shape[0], :, span], out, sems.at[index])
        first += out.shape[0]
        copy.start()
        copies.append(copy)
    for copy in copies:
        copy.wait()


def cut(at, loads, cols, counts, after):
    half = loads.shape[1]
    return pl.pallas_call(
        cut_kernel,
        in_specs=[SMEM, ANY, ANY],
        out_specs=[VMEM] * len(counts),
        out_shape=[jax.ShapeDtypeStruct((count, half, cols), F32) for count in counts],
        scratch_shapes=[pltpu.SemaphoreType.DMA((len(counts),))],
        compiler_params=params(4),
        cost_estimate=cost(1, 1 << 23),
        name="cut",
    )(at, in_hbm(loads), after)


def shards(size, panel, solved, loads, window, inverses):
    me = lax.axis_index("blk")
    side = lax.axis_index("rows").astype(jnp.int32)[None]
    bits = size.bit_length() - 1
    flags = [(me >> bit) & 1 for bit in range(bits)]
    step_count, half, _ = panel.shape
    block = inverses.shape[2]
    rhs = solved.shape[1]

    halvings = 1
    while halvings < bits and (rhs >> halvings) % (2 * LANES) == 0:
        halvings += 1
    inner = halvings - 1
    cols = rhs >> halvings
    blocks = 1 << halvings
    mine = sum(flags[bit] << (inner - bit) for bit in range(halvings))
    reverse = [sum(((mask >> bit) & 1) << (inner - bit) for bit in range(halvings)) for mask in range(blocks)]
    cross = [2 * mask for mask in range(1 << inner)]
    split_at = jnp.stack([(mine ^ reverse[mask]) & ((1 << inner) - 1) for mask in cross]).astype(jnp.int32)
    put_at = jnp.stack([mine ^ reverse[mask] for mask in cross + [mask + 1 for mask in cross]]).astype(jnp.int32)
    core = flags[0].astype(jnp.int32)[None]

    pair = [(0, 1), (1, 0)]
    first_count = (step_count + 1) // 2
    steps_a, steps_b = tuple(range(first_count)), tuple(range(first_count, step_count))
    shape = (step_count, half, rhs)
    units = far_units((steps_a, steps_b))
    together = lax.optimization_barrier

    def scatter(send, keep):
        pieces = split(split_at, keep, swap(send, "blk", size, 1), len(cross))
        return pieces[0], [swap(piece, "blk", size, mask) for mask, piece in zip(cross[1:], pieces[1:])], pieces[1]

    def collect(own, got):
        for piece in got:
            own = own + piece.astype(F32)
        part = own.astype(BF)
        for bit in range(halvings, bits - 1):
            part = (part.astype(F32) + swap(part, "blk", size, 1 << bit).astype(F32)).astype(BF)
        return part, swap(part, "blk", size, 1 << (bits - 1))

    def remain(load, part, got):
        return load - (part.astype(F32) + got.astype(F32)).reshape(load.shape)

    def spread(answer):
        return [swap(answer, "blk", size, mask) for mask in cross[1:]]

    def forward(answer, got):
        pieces = [answer] + got
        return pieces + [swap(piece, "blk", size, 1) for piece in pieces]

    send, keep = gemm(core, panel, solved, steps_a, [])
    sent = pack(units, core, inverses, window, send)
    here = lax.ppermute(sent, "rows", pair)
    own_a, got_a, after = scatter(send, keep)
    send, keep = gemm(core, panel, solved, steps_b, [after, sent])
    send, got_a = together((send, got_a))
    own_b, got_b, after = scatter(send, keep)
    load_a, load_b = cut(mine.astype(jnp.int32)[None], loads, cols, (len(steps_a), len(steps_b)), after)
    part_a, half_a = collect(own_a, got_a)
    here = anchor(here, [after])
    half_a = anchor(half_a, [load_a])
    got_b[-1] = anchor(got_b[-1], [half_a])
    part_b, half_b = collect(own_b, got_b)
    left_a = remain(load_a, part_a, half_a)
    far_a = lax.ppermute(left_a.astype(BF), "rows", pair)
    there = swap(here, "blk", size, 1)
    far_w = unpack(core, here, there)
    answer_a, known = chain(units, steps_a, side, inverses, window, far_w, left_a, far_a, [])
    got_a = spread(answer_a)
    load_b = couple(load_b, window, known)
    left_b = remain(load_b, part_b, anchor(half_b, [load_b]))
    far_b = lax.ppermute(left_b.astype(BF), "rows", pair)
    answer_b, _ = chain(units, steps_b, side, inverses, window, far_w, left_b, far_b, got_a)
    got_b = spread(answer_b)
    return put((steps_a[0], steps_b[0]), shape, put_at, forward(answer_a, got_a) + forward(answer_b, got_b))


def solution(mesh):
    placed = (
        P(None, "rows", "blk"),
        P("blk", None),
        P(None, "rows", None),
        P(None, "rows", None),
        P(None, "rows", None),
    )
    return jax.shard_map(
        functools.partial(shards, mesh.shape["blk"]),
        mesh=mesh,
        in_specs=placed,
        out_specs=P(None, "rows", None),
        check_vma=False,
    )
```

```python
import functools

import jax
import jax.numpy as jnp
from jax import lax
from jax.experimental import pallas as pl
from jax.experimental.pallas import tpu as pltpu
from jax.sharding import PartitionSpec as P

BF = jnp.bfloat16
F32 = jnp.float32
LANES = 128
MIB = 1 << 20
VMEM = pl.BlockSpec(memory_space=pltpu.VMEM)
SMEM = pl.BlockSpec(memory_space=pltpu.SMEM)
ANY = pl.BlockSpec(memory_space=pl.ANY)


def swap(value, axis, size, mask):
    return lax.ppermute(value, axis, [(i, i ^ mask) for i in range(size)])


def pick(flag, when_set, when_clear):
    return jnp.where(flag, when_set, when_clear)


def cost(flops, moved):
    return pl.CostEstimate(flops=flops, bytes_accessed=moved, transcendentals=0)


def in_hbm(value):
    return pltpu.with_memory_space_constraint(value, pltpu.HBM)


def params(mib):
    return pltpu.CompilerParams(vmem_limit_bytes=mib * MIB)


def halve(value, flag, send, keep):
    mid = send.shape[1]
    low, high = value[:, :mid], value[:, mid:]
    send[...] = jnp.where(flag, low, high).astype(send.dtype)
    keep[...] = jnp.where(flag, high, low).astype(keep.dtype)


def gemm_kernel(first, cuts, flag_ref, panel, solved, *refs):
    send, keep, rows, held, acc, sem_p, sem_s = refs[-7:]
    count, half, _ = rows.shape
    start = 0
    copies = []
    for index, cut in enumerate(cuts):
        span = slice(start, start + cut)
        start += cut
        copy_p = pltpu.make_async_copy(panel.at[first : first + count, :, span], rows.at[:, :, span], sem_p.at[index])
        copy_s = pltpu.make_async_copy(solved.at[span], held.at[span], sem_s.at[index])
        copy_p.start()
        copy_s.start()
        copies.append((span, copy_p, copy_s))
    flag = flag_ref[0] == 1
    for index, (span, copy_p, copy_s) in enumerate(copies):
        copy_p.wait()
        copy_s.wait()
        part = jnp.dot(
            rows[:, :, span].reshape(count * half, cuts[index]), held[span, :], preferred_element_type=F32
        )
        if index:
            part = part + acc[...]
        if index + 1 < len(cuts):
            acc[...] = part
        else:
            halve(part, flag, send, keep)


def gemm(flag, panel, solved, steps, after):
    _, half, depth = panel.shape
    rhs = solved.shape[1]
    count = len(steps)
    pieces = next(p for p in (6, 8, 4, 3, 2, 1) if depth % (p * LANES) == 0)
    cuts = (depth // pieces,) * pieces
    if cuts[0] % (2 * LANES) == 0:
        cuts = (cuts[0] // 2,) * 2 + cuts[1:]
    rows = count * half
    return pl.pallas_call(
        functools.partial(gemm_kernel, steps[0], cuts),
        in_specs=[SMEM, ANY, ANY] + [ANY] * len(after),
        out_specs=[VMEM] * 2,
        out_shape=[
            jax.ShapeDtypeStruct((rows, rhs // 2), BF),
            jax.ShapeDtypeStruct((rows, rhs // 2), BF),
        ],
        scratch_shapes=[
            pltpu.VMEM((count, half, depth), BF),
            pltpu.VMEM((depth, rhs), BF),
            pltpu.VMEM((rows, rhs), F32),
            pltpu.SemaphoreType.DMA((len(cuts),)),
            pltpu.SemaphoreType.DMA((len(cuts),)),
        ],
        compiler_params=params(30),
        cost_estimate=cost(1, 1),
        name="gemm",
    )(flag, in_hbm(panel), in_hbm(solved), *after)


def split_kernel(count, at_ref, keep, got, *refs):
    pieces = refs[-count:]
    width = pieces[0].shape[1]
    for index, piece in enumerate(pieces):
        span = pl.ds(pl.multiple_of(at_ref[index] * width, width), width)
        piece[...] = (keep[:, span].astype(F32) + got[:, span].astype(F32)).astype(piece.dtype)


def split(at, keep, got, count, after):
    rows, cols = keep.shape
    return pl.pallas_call(
        functools.partial(split_kernel, count),
        in_specs=[SMEM, VMEM, VMEM] + [ANY] * len(after),
        out_specs=[VMEM] * count,
        out_shape=[jax.ShapeDtypeStruct((rows, cols // count), BF if i else F32) for i in range(count)],
        compiler_params=params(16),
        name="split",
    )(at, keep, got, *after)


def far_units(groups):
    units = []
    for steps in groups:
        for step in steps:
            if step != groups[-1][-1]:
                units += [("inverses", step, piece) for piece in range(2)]
            units += [("window", step, piece) for piece in range(2 * steps[0], 2 * step)]
    return units


def pack_kernel(units, flag_ref, inverses, window, after, out, sems):
    del after
    half = out.shape[1]
    sources = {"inverses": inverses, "window": window}
    mid = out.shape[0]
    for core in range(2):

        @pl.when(flag_ref[0] == core)
        def _():
            copies = []
            for index, (name, step, piece) in enumerate(units[core * mid : (core + 1) * mid]):
                span = slice(piece * half, (piece + 1) * half)
                copy = pltpu.make_async_copy(sources[name].at[step, :, span], out.at[index], sems.at[index])
                copy.start()
                copies.append(copy)
            for copy in copies:
                copy.wait()


def pack(units, flag, inverses, window, after):
    half = inverses.shape[1]
    mid = (len(units) + 1) // 2
    return pl.pallas_call(
        functools.partial(pack_kernel, units),
        in_specs=[SMEM, ANY, ANY, ANY],
        out_specs=VMEM,
        out_shape=jax.ShapeDtypeStruct((mid, half, half), BF),
        scratch_shapes=[pltpu.SemaphoreType.DMA((mid,))],
        compiler_params=params(4),
        cost_estimate=cost(1, 4 * mid * half * half),
        name="pack",
    )(flag, in_hbm(inverses), in_hbm(window), after)


def unpack_kernel(flag_ref, here, there, out, sems):
    mid = here.shape[0]
    flag = flag_ref[0]
    copies = [
        pltpu.make_async_copy(here, out.at[pl.ds(flag * mid, mid)], sems.at[0]),
        pltpu.make_async_copy(there, out.at[pl.ds((1 - flag) * mid, mid)], sems.at[1]),
    ]
    for copy in copies:
        copy.start()
    for copy in copies:
        copy.wait()


def unpack(flag, here, there):
    mid, half, _ = here.shape
    return pl.pallas_call(
        unpack_kernel,
        in_specs=[SMEM, ANY, ANY],
        out_specs=VMEM,
        out_shape=jax.ShapeDtypeStruct((2 * mid, half, half), BF),
        scratch_shapes=[pltpu.SemaphoreType.DMA((2,))],
        compiler_params=params(4),
        cost_estimate=cost(1, 8 * mid * half * half),
        name="unpack",
    )(flag, here, there)


def chain_kernel(units, steps, last, waits, side_ref, inverses, far_w, own_r, far_r, *refs):
    _, half, block = inverses.shape
    start, count = steps[0], len(steps)
    if waits:
        inner = refs[0]
        own_out, right, solved = refs[-3:]
    else:
        window, later = refs[:2]
        own_out, later_out, right, solved, inner, outer, sems = refs[-7:]
        tiles = window.at[start + 1 : start + count, :, start * block : (start + count - 1) * block]
        fetch_inner = pltpu.make_async_copy(tiles, inner, sems.at[0])
        tiles = window.at[start + count :, :, start * block : (start + count) * block]
        fetch_outer = pltpu.make_async_copy(tiles, outer, sems.at[1])
        fetch_inner.start()
        fetch_outer.start()
    side = side_ref[0]
    near_at = pl.multiple_of(side * half, half)
    far_at = pl.multiple_of((1 - side) * half, half)
    for place, step in enumerate(steps):
        near = own_r[place].astype(F32)
        far = far_r[place].astype(F32)
        if place == 1 and not waits:
            fetch_inner.wait()
        if place:
            known = solved[: place * block, :]
            near = near - jnp.dot(inner[place - 1, :, : place * block], known, preferred_element_type=F32)
            for piece in range(2 * place):
                known = solved[piece * half : (piece + 1) * half, :]
                tile = far_w[units.index(("window", step, 2 * start + piece))]
                far = far - jnp.dot(tile, known, preferred_element_type=F32)
        right[pl.ds(near_at, half), :] = near.astype(BF)
        right[pl.ds(far_at, half), :] = far.astype(BF)
        near = jnp.dot(inverses[step], right[...], preferred_element_type=F32).astype(BF)
        own_out[place] = near
        if step != last:
            far = jnp.zeros_like(far)
            for piece in range(2):
                tile = far_w[units.index(("inverses", step, piece))]
                far = far + jnp.dot(tile, right[piece * half : (piece + 1) * half, :], preferred_element_type=F32)
            solved[pl.ds(pl.multiple_of(place * block + near_at, half), half), :] = near
            solved[pl.ds(pl.multiple_of(place * block + far_at, half), half), :] = far.astype(BF)
    if not waits:
        fetch_outer.wait()
        flat = outer[...].reshape(outer.shape[0] * half, count * block)
        taken = jnp.dot(flat, solved[...], preferred_element_type=F32)
        later_out[...] = later[...] - taken.reshape(later.shape)


def chain(units, steps, side, inverses, far_w, own_r, far_r, tiles, after):
    count, half, cols = own_r.shape
    block = 2 * half
    waits = len(tiles) == 1
    args = [side, inverses, far_w, own_r, far_r]
    outs = [jax.ShapeDtypeStruct((count, half, cols), BF)]
    scratch = [pltpu.VMEM((block, cols), BF), pltpu.VMEM((count * block, cols), BF)]
    if waits:
        specs = [VMEM]
    else:
        window, later = tiles
        tiles = [in_hbm(window), later]
        specs = [ANY, VMEM]
        outs.append(jax.ShapeDtypeStruct(later.shape, F32))
        scratch += [
            pltpu.VMEM((count - 1, half, (count - 1) * block), BF),
            pltpu.VMEM((later.shape[0], half, count * block), BF),
            pltpu.SemaphoreType.DMA((2,)),
        ]
    return pl.pallas_call(
        functools.partial(chain_kernel, units, steps, inverses.shape[0] - 1, waits),
        in_specs=[SMEM] + [VMEM] * (len(args) - 1) + specs + [ANY] * len(after),
        out_specs=[VMEM] * len(outs),
        out_shape=outs,
        scratch_shapes=scratch,
        compiler_params=params(12),
        name="chain",
    )(*args, *tiles, *after)


def fetch_kernel(first, column, window, after, out, sems):
    del after
    count, _, cols = out.shape
    copy = pltpu.make_async_copy(window.at[first : first + count, :, column : column + cols], out, sems.at[0])
    copy.start()
    copy.wait()


def fetch(window, steps, block, after):
    count, half = len(steps) - 1, window.shape[1]
    return pl.pallas_call(
        functools.partial(fetch_kernel, steps[1], steps[0] * block),
        in_specs=[ANY, ANY],
        out_specs=VMEM,
        out_shape=jax.ShapeDtypeStruct((count, half, count * block), BF),
        scratch_shapes=[pltpu.SemaphoreType.DMA((1,))],
        compiler_params=params(4),
        cost_estimate=cost(1, 1 << 22),
        name="fetch",
    )(in_hbm(window), after)


def anchor_kernel(*refs):
    del refs


def anchor(value, after):
    return pl.pallas_call(
        anchor_kernel,
        in_specs=[ANY] * (1 + len(after)),
        out_specs=ANY,
        out_shape=jax.ShapeDtypeStruct(value.shape, value.dtype),
        input_output_aliases={0: 0},
        compiler_params=params(1),
        cost_estimate=cost(1, 1),
        name="anchor",
    )(value, *after)


def put_kernel(firsts, at_ref, *refs):
    out, sems = refs[-2:]
    copies = []
    for index, (first, piece) in enumerate(zip(firsts, refs)):
        count, _, cols = piece.shape
        span = pl.ds(pl.multiple_of(at_ref[index] * cols, cols), cols)
        copies.append(pltpu.make_async_copy(piece, out.at[first : first + count, :, span], sems.at[index]))
        copies[-1].start()
    for copy in copies:
        copy.wait()


def put(shape, placed):
    firsts = [first for first, _, _ in placed]
    at = jnp.stack([column for _, column, _ in placed]).astype(jnp.int32)
    pieces = [piece for _, _, piece in placed]
    return pl.pallas_call(
        functools.partial(put_kernel, firsts),
        in_specs=[SMEM] + [VMEM] * len(pieces),
        out_specs=ANY,
        out_shape=jax.ShapeDtypeStruct(shape, BF),
        scratch_shapes=[pltpu.SemaphoreType.DMA((len(pieces),))],
        compiler_params=params(16),
        name="put",
    )(at, *pieces)


def cut_kernel(at_ref, loads, after, *refs):
    del after
    outs, sems = refs[:-1], refs[-1]
    cols = outs[0].shape[2]
    span = pl.ds(pl.multiple_of(at_ref[0] * cols, cols), cols)
    copies = []
    first = 0
    for index, out in enumerate(outs):
        copy = pltpu.make_async_copy(loads.at[first : first + out.shape[0], :, span], out, sems.at[index])
        first += out.shape[0]
        copy.start()
        copies.append(copy)
    for copy in copies:
        copy.wait()


def cut(at, loads, cols, counts, after):
    half = loads.shape[1]
    return pl.pallas_call(
        cut_kernel,
        in_specs=[SMEM, ANY, ANY],
        out_specs=[VMEM] * len(counts),
        out_shape=[jax.ShapeDtypeStruct((count, half, cols), F32) for count in counts],
        scratch_shapes=[pltpu.SemaphoreType.DMA((len(counts),))],
        compiler_params=params(4),
        cost_estimate=cost(1, 1 << 23),
        name="cut",
    )(at, in_hbm(loads), after)


def shards(size, panel, solved, loads, window, inverses):
    me = lax.axis_index("blk")
    side = lax.axis_index("rows").astype(jnp.int32)[None]
    bits = size.bit_length() - 1
    flags = [(me >> bit) & 1 for bit in range(bits)]
    step_count, half, _ = panel.shape
    block = inverses.shape[2]
    rhs = solved.shape[1]

    halvings = 1
    while halvings < bits and (rhs >> halvings) % (2 * LANES) == 0:
        halvings += 1
    inner = halvings - 1
    cols = rhs >> halvings
    blocks = 1 << halvings
    mine = sum(flags[bit] << (inner - bit) for bit in range(halvings))
    reverse = [sum(((mask >> bit) & 1) << (inner - bit) for bit in range(halvings)) for mask in range(blocks)]
    cross = [2 * mask for mask in range(1 << inner)]
    split_at = jnp.stack([(mine ^ reverse[mask]) & ((1 << inner) - 1) for mask in cross]).astype(jnp.int32)
    put_at = jnp.stack([mine ^ reverse[mask] for mask in cross + [mask + 1 for mask in cross]]).astype(jnp.int32)
    core = flags[0].astype(jnp.int32)[None]

    pair = [(0, 1), (1, 0)]
    first_count = (step_count + 1) // 2
    steps_a, steps_b = tuple(range(first_count)), tuple(range(first_count, step_count))
    shape = (step_count, half, rhs)
    units = far_units((steps_a, steps_b))
    together = lax.optimization_barrier

    def scatter(send, keep, after):
        pieces = split(split_at, keep, swap(send, "blk", size, 1), len(cross), after)
        return pieces[0], [swap(piece, "blk", size, mask) for mask, piece in zip(cross[1:], pieces[1:])], pieces[1]

    def collect(own, got):
        for piece in got:
            own = own + piece.astype(F32)
        part = own.astype(BF)
        for bit in range(halvings, bits - 1):
            part = (part.astype(F32) + swap(part, "blk", size, 1 << bit).astype(F32)).astype(BF)
        return part, swap(part, "blk", size, 1 << (bits - 1))

    def remain(load, part, got):
        return load - (part.astype(F32) + got.astype(F32)).reshape(load.shape)

    def spread(answer):
        return [swap(answer, "blk", size, mask) for mask in cross[1:]]

    def forward(answer, got):
        pieces = [answer] + got
        return pieces + [swap(piece, "blk", size, 1) for piece in pieces]

    send, keep = gemm(core, panel, solved, steps_a, [])
    sent = pack(units, core, inverses, window, send)
    here = lax.ppermute(sent, "rows", pair)
    own_a, got_a, after = scatter(send, keep, [sent])
    send, keep = gemm(core, panel, solved, steps_b, [after])
    send, got_a = together((send, got_a))
    own_b, got_b, after = scatter(send, keep, [])
    load_a, load_b = cut(mine.astype(jnp.int32)[None], loads, cols, (len(steps_a), len(steps_b)), after)
    part_a, half_a = collect(own_a, got_a)
    here = anchor(here, [after])
    half_a = anchor(half_a, [load_a])
    tiles_b = fetch(window, steps_b, block, load_a)
    got_b[-1] = anchor(got_b[-1], [half_a, tiles_b])
    part_b, half_b = collect(own_b, got_b)
    left_a = remain(load_a, part_a, half_a)
    far_a = lax.ppermute(left_a.astype(BF), "rows", pair)
    there = swap(here, "blk", size, 1)
    far_w = unpack(core, here, there)
    answer_a, load_b = chain(units, steps_a, side, inverses, far_w, left_a, far_a, [window, load_b], [])
    got_a = spread(answer_a)
    left_b = remain(load_b, part_b, anchor(half_b, [load_b]))
    rounded = left_b.astype(BF)
    far_b = lax.ppermute(rounded, "rows", pair)
    (answer_b,) = chain(units, steps_b, side, inverses, far_w, left_b, far_b, [tiles_b], got_a)
    got_b = spread(answer_b)
    pieces = [(steps_a[0], put_at[i], piece) for i, piece in enumerate(forward(answer_a, got_a))]
    pieces += [(steps_b[0], put_at[i], piece) for i, piece in enumerate(forward(answer_b, got_b))]
    return put(shape, pieces)


def solution(mesh):
    placed = (
        P(None, "rows", "blk"),
        P("blk", None),
        P(None, "rows", None),
        P(None, "rows", None),
        P(None, "rows", None),
    )
    return jax.shard_map(
        functools.partial(shards, mesh.shape["blk"]),
        mesh=mesh,
        in_specs=placed,
        out_specs=P(None, "rows", None),
        check_vma=False,
    )
```

```python
import functools

import jax
import jax.numpy as jnp
from jax import lax
from jax.experimental import pallas as pl
from jax.experimental.pallas import tpu as pltpu
from jax.sharding import PartitionSpec as P

BF = jnp.bfloat16
F32 = jnp.float32
LANES = 128
MIB = 1 << 20
VMEM = pl.BlockSpec(memory_space=pltpu.VMEM)
SMEM = pl.BlockSpec(memory_space=pltpu.SMEM)
ANY = pl.BlockSpec(memory_space=pl.ANY)


def swap(value, axis, size, mask):
    return lax.ppermute(value, axis, [(i, i ^ mask) for i in range(size)])


def cost(flops, moved):
    return pl.CostEstimate(flops=flops, bytes_accessed=moved, transcendentals=0)


def in_hbm(value):
    return pltpu.with_memory_space_constraint(value, pltpu.HBM)


def params(mib):
    return pltpu.CompilerParams(vmem_limit_bytes=mib * MIB)


def halve(value, flag, send, keep):
    mid = send.shape[1]
    low, high = value[:, :mid], value[:, mid:]
    send[...] = jnp.where(flag, low, high).astype(send.dtype)
    keep[...] = jnp.where(flag, high, low).astype(keep.dtype)


def gemm_kernel(first, cuts, flag_ref, panel, solved, *refs):
    send, keep, rows, held, acc, sem_p, sem_s = refs[-7:]
    count, half, _ = rows.shape
    start = 0
    copies = []
    for index, cut in enumerate(cuts):
        span = slice(start, start + cut)
        start += cut
        copy_p = pltpu.make_async_copy(panel.at[first : first + count, :, span], rows.at[:, :, span], sem_p.at[index])
        copy_s = pltpu.make_async_copy(solved.at[span], held.at[span], sem_s.at[index])
        copy_p.start()
        copy_s.start()
        copies.append((span, copy_p, copy_s))
    flag = flag_ref[0] == 1
    for index, (span, copy_p, copy_s) in enumerate(copies):
        copy_p.wait()
        copy_s.wait()
        part = jnp.dot(
            rows[:, :, span].reshape(count * half, cuts[index]), held[span, :], preferred_element_type=F32
        )
        if index:
            part = part + acc[...]
        if index + 1 < len(cuts):
            acc[...] = part
        else:
            halve(part, flag, send, keep)


def gemm(flag, panel, solved, steps, after):
    _, half, depth = panel.shape
    rhs = solved.shape[1]
    count = len(steps)
    pieces = next(p for p in (6, 8, 4, 3, 2, 1) if depth % (p * LANES) == 0)
    cuts = (depth // pieces,) * pieces
    if cuts[0] % (2 * LANES) == 0:
        cuts = (cuts[0] // 2,) * 2 + cuts[1:]
    rows = count * half
    return pl.pallas_call(
        functools.partial(gemm_kernel, steps[0], cuts),
        in_specs=[SMEM, ANY, ANY] + [ANY] * len(after),
        out_specs=[VMEM] * 2,
        out_shape=[
            jax.ShapeDtypeStruct((rows, rhs // 2), BF),
            jax.ShapeDtypeStruct((rows, rhs // 2), BF),
        ],
        scratch_shapes=[
            pltpu.VMEM((count, half, depth), BF),
            pltpu.VMEM((depth, rhs), BF),
            pltpu.VMEM((rows, rhs), F32),
            pltpu.SemaphoreType.DMA((len(cuts),)),
            pltpu.SemaphoreType.DMA((len(cuts),)),
        ],
        compiler_params=params(30),
        cost_estimate=cost(1, 1),
        name="gemm",
    )(flag, in_hbm(panel), in_hbm(solved), *after)


def split_kernel(count, at_ref, keep, got, *refs):
    pieces = refs[-count:]
    width = pieces[0].shape[1]
    for index, piece in enumerate(pieces):
        span = pl.ds(pl.multiple_of(at_ref[index] * width, width), width)
        piece[...] = (keep[:, span].astype(F32) + got[:, span].astype(F32)).astype(piece.dtype)


def split(at, keep, got, count, after):
    rows, cols = keep.shape
    return pl.pallas_call(
        functools.partial(split_kernel, count),
        in_specs=[SMEM, VMEM, VMEM] + [ANY] * len(after),
        out_specs=[VMEM] * count,
        out_shape=[jax.ShapeDtypeStruct((rows, cols // count), BF if i else F32) for i in range(count)],
        compiler_params=params(16),
        name="split",
    )(at, keep, got, *after)


def far_units(groups):
    units = []
    for steps in groups:
        for step in steps:
            if step != groups[-1][-1]:
                units += [("inverses", step, piece) for piece in range(2)]
            units += [("window", step, piece) for piece in range(2 * steps[0], 2 * step)]
    return units


def pack_kernel(units, flag_ref, inverses, window, after, out, sems):
    del after
    half = out.shape[1]
    sources = {"inverses": inverses, "window": window}
    mid = out.shape[0]
    for core in range(2):

        @pl.when(flag_ref[0] == core)
        def _():
            copies = []
            for index, (name, step, piece) in enumerate(units[core * mid : (core + 1) * mid]):
                span = slice(piece * half, (piece + 1) * half)
                copy = pltpu.make_async_copy(sources[name].at[step, :, span], out.at[index], sems.at[index])
                copy.start()
                copies.append(copy)
            for copy in copies:
                copy.wait()


def pack(units, flag, inverses, window, after):
    half = inverses.shape[1]
    mid = (len(units) + 1) // 2
    return pl.pallas_call(
        functools.partial(pack_kernel, units),
        in_specs=[SMEM, ANY, ANY, ANY],
        out_specs=VMEM,
        out_shape=jax.ShapeDtypeStruct((mid, half, half), BF),
        scratch_shapes=[pltpu.SemaphoreType.DMA((mid,))],
        compiler_params=params(4),
        cost_estimate=cost(1, 4 * mid * half * half),
        name="pack",
    )(flag, in_hbm(inverses), in_hbm(window), after)


def unpack_kernel(flag_ref, here, there, out, sems):
    mid = here.shape[0]
    flag = flag_ref[0]
    copies = [
        pltpu.make_async_copy(here, out.at[pl.ds(flag * mid, mid)], sems.at[0]),
        pltpu.make_async_copy(there, out.at[pl.ds((1 - flag) * mid, mid)], sems.at[1]),
    ]
    for copy in copies:
        copy.start()
    for copy in copies:
        copy.wait()


def unpack(flag, here, there):
    mid, half, _ = here.shape
    return pl.pallas_call(
        unpack_kernel,
        in_specs=[SMEM, ANY, ANY],
        out_specs=VMEM,
        out_shape=jax.ShapeDtypeStruct((2 * mid, half, half), BF),
        scratch_shapes=[pltpu.SemaphoreType.DMA((2,))],
        compiler_params=params(4),
        cost_estimate=cost(1, 8 * mid * half * half),
        name="unpack",
    )(flag, here, there)


def chain_kernel(units, steps, last, waits, side_ref, inverses, far_w, own_r, far_r, *refs):
    _, half, block = inverses.shape
    start, count = steps[0], len(steps)
    if waits:
        inner = refs[0]
        own_out, right, solved = refs[-3:]
    else:
        window, later = refs[:2]
        own_out, later_out, right, solved, inner, outer, sems = refs[-7:]
        tiles = window.at[start + 1 : start + count, :, start * block : (start + count - 1) * block]
        fetch_inner = pltpu.make_async_copy(tiles, inner, sems.at[0])
        tiles = window.at[start + count :, :, start * block : (start + count) * block]
        fetch_outer = pltpu.make_async_copy(tiles, outer, sems.at[1])
        fetch_inner.start()
        fetch_outer.start()
    side = side_ref[0]
    near_at = pl.multiple_of(side * half, half)
    far_at = pl.multiple_of((1 - side) * half, half)
    for place, step in enumerate(steps):
        near = own_r[place].astype(F32)
        far = far_r[place].astype(F32)
        if place == 1 and not waits:
            fetch_inner.wait()
        if place:
            known = solved[: place * block, :]
            near = near - jnp.dot(inner[place - 1, :, : place * block], known, preferred_element_type=F32)
            for piece in range(2 * place):
                known = solved[piece * half : (piece + 1) * half, :]
                tile = far_w[units.index(("window", step, 2 * start + piece))]
                far = far - jnp.dot(tile, known, preferred_element_type=F32)
        right[pl.ds(near_at, half), :] = near.astype(BF)
        right[pl.ds(far_at, half), :] = far.astype(BF)
        near = jnp.dot(inverses[step], right[...], preferred_element_type=F32).astype(BF)
        own_out[place] = near
        if step != last:
            far = jnp.zeros_like(far)
            for piece in range(2):
                tile = far_w[units.index(("inverses", step, piece))]
                far = far + jnp.dot(tile, right[piece * half : (piece + 1) * half, :], preferred_element_type=F32)
            solved[pl.ds(pl.multiple_of(place * block + near_at, half), half), :] = near
            solved[pl.ds(pl.multiple_of(place * block + far_at, half), half), :] = far.astype(BF)
    if not waits:
        fetch_outer.wait()
        flat = outer[...].reshape(outer.shape[0] * half, count * block)
        taken = jnp.dot(flat, solved[...], preferred_element_type=F32)
        later_out[...] = later[...] - taken.reshape(later.shape)


def chain(units, steps, side, inverses, far_w, own_r, far_r, tiles, after):
    count, half, cols = own_r.shape
    block = 2 * half
    waits = len(tiles) == 1
    args = [side, inverses, far_w, own_r, far_r]
    outs = [jax.ShapeDtypeStruct((count, half, cols), BF)]
    scratch = [pltpu.VMEM((block, cols), BF), pltpu.VMEM((count * block, cols), BF)]
    if waits:
        specs = [VMEM]
    else:
        window, later = tiles
        tiles = [in_hbm(window), later]
        specs = [ANY, VMEM]
        outs.append(jax.ShapeDtypeStruct(later.shape, F32))
        scratch += [
            pltpu.VMEM((count - 1, half, (count - 1) * block), BF),
            pltpu.VMEM((later.shape[0], half, count * block), BF),
            pltpu.SemaphoreType.DMA((2,)),
        ]
    return pl.pallas_call(
        functools.partial(chain_kernel, units, steps, inverses.shape[0] - 1, waits),
        in_specs=[SMEM] + [VMEM] * (len(args) - 1) + specs + [ANY] * len(after),
        out_specs=[VMEM] * len(outs),
        out_shape=outs,
        scratch_shapes=scratch,
        compiler_params=params(12),
        name="chain",
    )(*args, *tiles, *after)


def fetch_kernel(first, column, window, after, out, sems):
    del after
    count, _, cols = out.shape
    copy = pltpu.make_async_copy(window.at[first : first + count, :, column : column + cols], out, sems.at[0])
    copy.start()
    copy.wait()


def fetch(window, steps, block, after):
    count, half = len(steps) - 1, window.shape[1]
    return pl.pallas_call(
        functools.partial(fetch_kernel, steps[1], steps[0] * block),
        in_specs=[ANY, ANY],
        out_specs=VMEM,
        out_shape=jax.ShapeDtypeStruct((count, half, count * block), BF),
        scratch_shapes=[pltpu.SemaphoreType.DMA((1,))],
        compiler_params=params(4),
        cost_estimate=cost(1, 1 << 22),
        name="fetch",
    )(in_hbm(window), after)


def anchor_kernel(*refs):
    del refs


def anchor(value, after):
    return pl.pallas_call(
        anchor_kernel,
        in_specs=[ANY] * (1 + len(after)),
        out_specs=ANY,
        out_shape=jax.ShapeDtypeStruct(value.shape, value.dtype),
        input_output_aliases={0: 0},
        compiler_params=params(1),
        cost_estimate=cost(1, 1),
        name="anchor",
    )(value, *after)


def put_kernel(firsts, at_ref, *refs):
    out, sems = refs[-2:]
    copies = []
    for index, (first, piece) in enumerate(zip(firsts, refs)):
        count, _, cols = piece.shape
        span = pl.ds(pl.multiple_of(at_ref[index] * cols, cols), cols)
        copies.append(pltpu.make_async_copy(piece, out.at[first : first + count, :, span], sems.at[index]))
        copies[-1].start()
    for copy in copies:
        copy.wait()


def put(shape, placed):
    firsts = [first for first, _, _ in placed]
    at = jnp.stack([column for _, column, _ in placed]).astype(jnp.int32)
    pieces = [piece for _, _, piece in placed]
    return pl.pallas_call(
        functools.partial(put_kernel, firsts),
        in_specs=[SMEM] + [VMEM] * len(pieces),
        out_specs=ANY,
        out_shape=jax.ShapeDtypeStruct(shape, BF),
        scratch_shapes=[pltpu.SemaphoreType.DMA((len(pieces),))],
        compiler_params=params(16),
        name="put",
    )(at, *pieces)


def cut_kernel(at_ref, loads, after, *refs):
    del after
    outs, sems = refs[:-1], refs[-1]
    cols = outs[0].shape[2]
    span = pl.ds(pl.multiple_of(at_ref[0] * cols, cols), cols)
    copies = []
    first = 0
    for index, out in enumerate(outs):
        copy = pltpu.make_async_copy(loads.at[first : first + out.shape[0], :, span], out, sems.at[index])
        first += out.shape[0]
        copy.start()
        copies.append(copy)
    for copy in copies:
        copy.wait()


def cut(at, loads, cols, counts, after):
    half = loads.shape[1]
    return pl.pallas_call(
        cut_kernel,
        in_specs=[SMEM, ANY, ANY],
        out_specs=[VMEM] * len(counts),
        out_shape=[jax.ShapeDtypeStruct((count, half, cols), F32) for count in counts],
        scratch_shapes=[pltpu.SemaphoreType.DMA((len(counts),))],
        compiler_params=params(4),
        cost_estimate=cost(1, 1 << 23),
        name="cut",
    )(at, in_hbm(loads), after)


def shards(size, panel, solved, loads, window, inverses):
    me = lax.axis_index("blk")
    side = lax.axis_index("rows").astype(jnp.int32)[None]
    bits = size.bit_length() - 1
    flags = [(me >> bit) & 1 for bit in range(bits)]
    step_count, half, _ = panel.shape
    block = inverses.shape[2]
    rhs = solved.shape[1]

    halvings = 1
    while halvings < bits and (rhs >> halvings) % (2 * LANES) == 0:
        halvings += 1
    inner = halvings - 1
    cols = rhs >> halvings
    blocks = 1 << halvings
    mine = sum(flags[bit] << (inner - bit) for bit in range(halvings))
    reverse = [sum(((mask >> bit) & 1) << (inner - bit) for bit in range(halvings)) for mask in range(blocks)]
    gray = [2 * (i ^ (i >> 1)) for i in range(1 << inner)]
    cross = gray[:1] + gray[:0:-1]
    split_at = jnp.stack([(mine ^ reverse[mask]) & ((1 << inner) - 1) for mask in cross]).astype(jnp.int32)
    put_at = jnp.stack([mine ^ reverse[mask] for mask in cross + [mask + 1 for mask in cross]]).astype(jnp.int32)
    core = flags[0].astype(jnp.int32)[None]

    pair = [(0, 1), (1, 0)]
    first_count = (step_count + 1) // 2
    steps_a, steps_b = tuple(range(first_count)), tuple(range(first_count, step_count))
    shape = (step_count, half, rhs)
    units = far_units((steps_a, steps_b))
    together = lax.optimization_barrier

    def scatter(send, keep, after):
        pieces = split(split_at, keep, swap(send, "blk", size, 1), len(cross), after)
        return pieces[0], [swap(piece, "blk", size, mask) for mask, piece in zip(cross[1:], pieces[1:])], pieces[1]

    def collect(own, got):
        for piece in got:
            own = own + piece.astype(F32)
        part = own.astype(BF)
        for bit in range(halvings, bits - 1):
            part = (part.astype(F32) + swap(part, "blk", size, 1 << bit).astype(F32)).astype(BF)
        return part, swap(part, "blk", size, 1 << (bits - 1))

    def remain(load, part, got):
        return load - (part.astype(F32) + got.astype(F32)).reshape(load.shape)

    def spread(answer):
        return [swap(answer, "blk", size, mask) for mask in cross[1:]]

    def forward(answer, got):
        pieces = [answer] + got
        return pieces + [swap(piece, "blk", size, 1) for piece in pieces]

    send, keep = gemm(core, panel, solved, steps_a, [])
    sent = pack(units, core, inverses, window, send)
    here = lax.ppermute(sent, "rows", pair)
    own_a, got_a, after = scatter(send, keep, [sent])
    send, keep = gemm(core, panel, solved, steps_b, [after])
    send, got_a = together((send, got_a))
    own_b, got_b, after = scatter(send, keep, [])
    load_a, load_b = cut(mine.astype(jnp.int32)[None], loads, cols, (len(steps_a), len(steps_b)), after)
    part_a, half_a = collect(own_a, got_a)
    here = anchor(here, [after])
    half_a = anchor(half_a, [load_a])
    tiles_b = fetch(window, steps_b, block, load_a)
    got_b[-1] = anchor(got_b[-1], [half_a, tiles_b])
    part_b, half_b = collect(own_b, got_b)
    left_a = remain(load_a, part_a, half_a)
    far_a = lax.ppermute(left_a.astype(BF), "rows", pair)
    there = swap(here, "blk", size, 1)
    far_w = unpack(core, here, there)
    answer_a, load_b = chain(units, steps_a, side, inverses, far_w, left_a, far_a, [window, load_b], [])
    got_a = spread(answer_a)
    left_b = remain(load_b, part_b, anchor(half_b, [load_b]))
    rounded = left_b.astype(BF)
    far_b = lax.ppermute(rounded, "rows", pair)
    (answer_b,) = chain(units, steps_b, side, inverses, far_w, left_b, far_b, [tiles_b], got_a)
    got_b = spread(answer_b)
    pieces = [(steps_a[0], put_at[i], piece) for i, piece in enumerate(forward(answer_a, got_a))]
    pieces += [(steps_b[0], put_at[i], piece) for i, piece in enumerate(forward(answer_b, got_b))]
    return put(shape, pieces)


def solution(mesh):
    placed = (
        P(None, "rows", "blk"),
        P("blk", None),
        P(None, "rows", None),
        P(None, "rows", None),
        P(None, "rows", None),
    )
    return jax.shard_map(
        functools.partial(shards, mesh.shape["blk"]),
        mesh=mesh,
        in_specs=placed,
        out_specs=P(None, "rows", None),
        check_vma=False,
    )
```

```python
import functools

import jax
import jax.numpy as jnp
from jax import lax
from jax.experimental import pallas as pl
from jax.experimental.pallas import tpu as pltpu
from jax.sharding import PartitionSpec as P

BF = jnp.bfloat16
F32 = jnp.float32
LANES = 128
MIB = 1 << 20
VMEM = pl.BlockSpec(memory_space=pltpu.VMEM)
SMEM = pl.BlockSpec(memory_space=pltpu.SMEM)
ANY = pl.BlockSpec(memory_space=pl.ANY)


def swap(value, axis, size, mask):
    return lax.ppermute(value, axis, [(i, i ^ mask) for i in range(size)])


def cost(flops, moved):
    return pl.CostEstimate(flops=flops, bytes_accessed=moved, transcendentals=0)


def in_hbm(value):
    return pltpu.with_memory_space_constraint(value, pltpu.HBM)


def params(mib):
    return pltpu.CompilerParams(vmem_limit_bytes=mib * MIB)


def halve(value, flag, send, keep):
    mid = send.shape[1]
    low, high = value[:, :mid], value[:, mid:]
    send[...] = jnp.where(flag, low, high).astype(send.dtype)
    keep[...] = jnp.where(flag, high, low).astype(keep.dtype)


def gemm_kernel(first, cuts, flag_ref, panel, solved, *refs):
    send, keep, rows, held, acc, sem_p, sem_s = refs[-7:]
    count, half, _ = rows.shape
    start = 0
    copies = []
    for index, cut in enumerate(cuts):
        span = slice(start, start + cut)
        start += cut
        copy_p = pltpu.make_async_copy(panel.at[first : first + count, :, span], rows.at[:, :, span], sem_p.at[index])
        copy_s = pltpu.make_async_copy(solved.at[span], held.at[span], sem_s.at[index])
        copy_p.start()
        copy_s.start()
        copies.append((span, copy_p, copy_s))
    flag = flag_ref[0] == 1
    for index, (span, copy_p, copy_s) in enumerate(copies):
        copy_p.wait()
        copy_s.wait()
        part = jnp.dot(
            rows[:, :, span].reshape(count * half, cuts[index]), held[span, :], preferred_element_type=F32
        )
        if index:
            part = part + acc[...]
        if index + 1 < len(cuts):
            acc[...] = part
        else:
            halve(part, flag, send, keep)


def gemm(flag, panel, solved, steps, after):
    _, half, depth = panel.shape
    rhs = solved.shape[1]
    count = len(steps)
    pieces = next(p for p in (6, 8, 4, 3, 2, 1) if depth % (p * LANES) == 0)
    cuts = (depth // pieces,) * pieces
    if cuts[0] % (2 * LANES) == 0:
        cuts = (cuts[0] // 2,) * 2 + cuts[1:]
    rows = count * half
    return pl.pallas_call(
        functools.partial(gemm_kernel, steps[0], cuts),
        in_specs=[SMEM, ANY, ANY] + [ANY] * len(after),
        out_specs=[VMEM] * 2,
        out_shape=[
            jax.ShapeDtypeStruct((rows, rhs // 2), BF),
            jax.ShapeDtypeStruct((rows, rhs // 2), BF),
        ],
        scratch_shapes=[
            pltpu.VMEM((count, half, depth), BF),
            pltpu.VMEM((depth, rhs), BF),
            pltpu.VMEM((rows, rhs), F32),
            pltpu.SemaphoreType.DMA((len(cuts),)),
            pltpu.SemaphoreType.DMA((len(cuts),)),
        ],
        compiler_params=params(30),
        cost_estimate=cost(1, 1),
        name="gemm",
    )(flag, in_hbm(panel), in_hbm(solved), *after)


def split_kernel(count, at_ref, keep, got, *refs):
    pieces = refs[-count:]
    width = pieces[0].shape[1]
    for index, piece in enumerate(pieces):
        span = pl.ds(pl.multiple_of(at_ref[index] * width, width), width)
        piece[...] = (keep[:, span].astype(F32) + got[:, span].astype(F32)).astype(piece.dtype)


def split(at, keep, got, count, after):
    rows, cols = keep.shape
    return pl.pallas_call(
        functools.partial(split_kernel, count),
        in_specs=[SMEM, VMEM, VMEM] + [ANY] * len(after),
        out_specs=[VMEM] * count,
        out_shape=[jax.ShapeDtypeStruct((rows, cols // count), BF if i else F32) for i in range(count)],
        compiler_params=params(16),
        name="split",
    )(at, keep, got, *after)


def far_units(groups):
    units = []
    for steps in groups:
        for step in steps:
            if step != groups[-1][-1]:
                units += [("inverses", step, piece) for piece in range(2)]
            units += [("window", step, piece) for piece in range(2 * steps[0], 2 * step)]
    return units


def pack_kernel(units, flag_ref, inverses, window, after, out, sems):
    del after
    half = out.shape[1]
    sources = {"inverses": inverses, "window": window}
    mid = out.shape[0]
    for core in range(2):

        @pl.when(flag_ref[0] == core)
        def _():
            copies = []
            for index, (name, step, piece) in enumerate(units[core * mid : (core + 1) * mid]):
                span = slice(piece * half, (piece + 1) * half)
                copy = pltpu.make_async_copy(sources[name].at[step, :, span], out.at[index], sems.at[index])
                copy.start()
                copies.append(copy)
            for copy in copies:
                copy.wait()


def pack(units, flag, inverses, window, after):
    half = inverses.shape[1]
    mid = (len(units) + 1) // 2
    return pl.pallas_call(
        functools.partial(pack_kernel, units),
        in_specs=[SMEM, ANY, ANY, ANY],
        out_specs=VMEM,
        out_shape=jax.ShapeDtypeStruct((mid, half, half), BF),
        scratch_shapes=[pltpu.SemaphoreType.DMA((mid,))],
        compiler_params=params(4),
        cost_estimate=cost(1, 4 * mid * half * half),
        name="pack",
    )(flag, in_hbm(inverses), in_hbm(window), after)


def unpack_kernel(flag_ref, here, there, out, sems):
    mid = here.shape[0]
    flag = flag_ref[0]
    copies = [
        pltpu.make_async_copy(here, out.at[pl.ds(flag * mid, mid)], sems.at[0]),
        pltpu.make_async_copy(there, out.at[pl.ds((1 - flag) * mid, mid)], sems.at[1]),
    ]
    for copy in copies:
        copy.start()
    for copy in copies:
        copy.wait()


def unpack(flag, here, there):
    mid, half, _ = here.shape
    return pl.pallas_call(
        unpack_kernel,
        in_specs=[SMEM, ANY, ANY],
        out_specs=VMEM,
        out_shape=jax.ShapeDtypeStruct((2 * mid, half, half), BF),
        scratch_shapes=[pltpu.SemaphoreType.DMA((2,))],
        compiler_params=params(4),
        cost_estimate=cost(1, 8 * mid * half * half),
        name="unpack",
    )(flag, here, there)


def chain_kernel(units, steps, last, waits, side_ref, inverses, far_w, own_r, far_r, *refs):
    _, half, block = inverses.shape
    start, count = steps[0], len(steps)
    if waits:
        inner = refs[0]
        own_out, right, solved = refs[-3:]
    else:
        window, later = refs[:2]
        own_out, later_out, right, solved, inner, outer, sems = refs[-7:]
        tiles = window.at[start + 1 : start + count, :, start * block : (start + count - 1) * block]
        fetch_inner = pltpu.make_async_copy(tiles, inner, sems.at[0])
        tiles = window.at[start + count :, :, start * block : (start + count) * block]
        fetch_outer = pltpu.make_async_copy(tiles, outer, sems.at[1])
        fetch_inner.start()
        fetch_outer.start()
    side = side_ref[0]
    near_at = pl.multiple_of(side * half, half)
    far_at = pl.multiple_of((1 - side) * half, half)
    for place, step in enumerate(steps):
        near = own_r[place].astype(F32)
        far = far_r[place].astype(F32)
        if place == 1 and not waits:
            fetch_inner.wait()
        if place:
            known = solved[: place * block, :]
            near = near - jnp.dot(inner[place - 1, :, : place * block], known, preferred_element_type=F32)
            for piece in range(2 * place):
                known = solved[piece * half : (piece + 1) * half, :]
                tile = far_w[units.index(("window", step, 2 * start + piece))]
                far = far - jnp.dot(tile, known, preferred_element_type=F32)
        right[pl.ds(near_at, half), :] = near.astype(BF)
        right[pl.ds(far_at, half), :] = far.astype(BF)
        near = jnp.dot(inverses[step], right[...], preferred_element_type=F32).astype(BF)
        own_out[place] = near
        if step != last:
            far = jnp.zeros_like(far)
            for piece in range(2):
                tile = far_w[units.index(("inverses", step, piece))]
                far = far + jnp.dot(tile, right[piece * half : (piece + 1) * half, :], preferred_element_type=F32)
            solved[pl.ds(pl.multiple_of(place * block + near_at, half), half), :] = near
            solved[pl.ds(pl.multiple_of(place * block + far_at, half), half), :] = far.astype(BF)
    if not waits:
        fetch_outer.wait()
        flat = outer[...].reshape(outer.shape[0] * half, count * block)
        taken = jnp.dot(flat, solved[...], preferred_element_type=F32)
        later_out[...] = later[...] - taken.reshape(later.shape)


def chain(units, steps, side, inverses, far_w, own_r, far_r, tiles, after):
    count, half, cols = own_r.shape
    block = 2 * half
    waits = len(tiles) == 1
    args = [side, inverses, far_w, own_r, far_r]
    outs = [jax.ShapeDtypeStruct((count, half, cols), BF)]
    scratch = [pltpu.VMEM((block, cols), BF), pltpu.VMEM((count * block, cols), BF)]
    if waits:
        specs = [VMEM]
    else:
        window, later = tiles
        tiles = [in_hbm(window), later]
        specs = [ANY, VMEM]
        outs.append(jax.ShapeDtypeStruct(later.shape, F32))
        scratch += [
            pltpu.VMEM((count - 1, half, (count - 1) * block), BF),
            pltpu.VMEM((later.shape[0], half, count * block), BF),
            pltpu.SemaphoreType.DMA((2,)),
        ]
    return pl.pallas_call(
        functools.partial(chain_kernel, units, steps, inverses.shape[0] - 1, waits),
        in_specs=[SMEM] + [VMEM] * (len(args) - 1) + specs + [ANY] * len(after),
        out_specs=[VMEM] * len(outs),
        out_shape=outs,
        scratch_shapes=scratch,
        compiler_params=params(12),
        name="chain",
    )(*args, *tiles, *after)


def fetch_kernel(first, column, window, after, out, sems):
    del after
    count, _, cols = out.shape
    copy = pltpu.make_async_copy(window.at[first : first + count, :, column : column + cols], out, sems.at[0])
    copy.start()
    copy.wait()


def fetch(window, steps, block, after):
    count, half = len(steps) - 1, window.shape[1]
    return pl.pallas_call(
        functools.partial(fetch_kernel, steps[1], steps[0] * block),
        in_specs=[ANY, ANY],
        out_specs=VMEM,
        out_shape=jax.ShapeDtypeStruct((count, half, count * block), BF),
        scratch_shapes=[pltpu.SemaphoreType.DMA((1,))],
        compiler_params=params(4),
        cost_estimate=cost(1, 1 << 22),
        name="fetch",
    )(in_hbm(window), after)


def anchor_kernel(*refs):
    del refs


def anchor(value, after):
    return pl.pallas_call(
        anchor_kernel,
        in_specs=[ANY] * (1 + len(after)),
        out_specs=ANY,
        out_shape=jax.ShapeDtypeStruct(value.shape, value.dtype),
        input_output_aliases={0: 0},
        compiler_params=params(1),
        cost_estimate=cost(1, 1),
        name="anchor",
    )(value, *after)


def put_kernel(firsts, at_ref, *refs):
    out, sems = refs[-2:]
    copies = []
    for index, (first, piece) in enumerate(zip(firsts, refs)):
        count, _, cols = piece.shape
        span = pl.ds(pl.multiple_of(at_ref[index] * cols, cols), cols)
        copies.append(pltpu.make_async_copy(piece, out.at[first : first + count, :, span], sems.at[index]))
        copies[-1].start()
    for copy in copies:
        copy.wait()


def put(shape, placed):
    firsts = [first for first, _, _ in placed]
    at = jnp.stack([column for _, column, _ in placed]).astype(jnp.int32)
    pieces = [piece for _, _, piece in placed]
    return pl.pallas_call(
        functools.partial(put_kernel, firsts),
        in_specs=[SMEM] + [VMEM] * len(pieces),
        out_specs=ANY,
        out_shape=jax.ShapeDtypeStruct(shape, BF),
        scratch_shapes=[pltpu.SemaphoreType.DMA((len(pieces),))],
        compiler_params=params(16),
        name="put",
    )(at, *pieces)


def cut_kernel(at_ref, loads, after, *refs):
    del after
    outs, sems = refs[:-1], refs[-1]
    cols = outs[0].shape[2]
    span = pl.ds(pl.multiple_of(at_ref[0] * cols, cols), cols)
    copies = []
    first = 0
    for index, out in enumerate(outs):
        copy = pltpu.make_async_copy(loads.at[first : first + out.shape[0], :, span], out, sems.at[index])
        first += out.shape[0]
        copy.start()
        copies.append(copy)
    for copy in copies:
        copy.wait()


def cut(at, loads, cols, counts, after):
    half = loads.shape[1]
    return pl.pallas_call(
        cut_kernel,
        in_specs=[SMEM, ANY, ANY],
        out_specs=[VMEM] * len(counts),
        out_shape=[jax.ShapeDtypeStruct((count, half, cols), F32) for count in counts],
        scratch_shapes=[pltpu.SemaphoreType.DMA((len(counts),))],
        compiler_params=params(4),
        cost_estimate=cost(1, 1 << 23),
        name="cut",
    )(at, in_hbm(loads), after)


def shards(size, panel, solved, loads, window, inverses):
    me = lax.axis_index("blk")
    side = lax.axis_index("rows").astype(jnp.int32)[None]
    bits = size.bit_length() - 1
    flags = [(me >> bit) & 1 for bit in range(bits)]
    step_count, half, _ = panel.shape
    block = inverses.shape[2]
    rhs = solved.shape[1]

    halvings = 1
    while halvings < bits and (rhs >> halvings) % (2 * LANES) == 0:
        halvings += 1
    inner = halvings - 1
    cols = rhs >> halvings
    blocks = 1 << halvings
    mine = sum(flags[bit] << (inner - bit) for bit in range(halvings))
    reverse = [sum(((mask >> bit) & 1) << (inner - bit) for bit in range(halvings)) for mask in range(blocks)]
    gray = [2 * (i ^ (i >> 1)) for i in range(1 << inner)]
    cross = gray[:1] + gray[:0:-1]
    outward = cross[:1] + sorted(cross[1:], reverse=True)
    split_at = jnp.stack([(mine ^ reverse[mask]) & ((1 << inner) - 1) for mask in outward]).astype(jnp.int32)
    put_at = jnp.stack([mine ^ reverse[mask] for mask in cross + [mask + 1 for mask in cross]]).astype(jnp.int32)
    core = flags[0].astype(jnp.int32)[None]

    pair = [(0, 1), (1, 0)]
    first_count = (step_count + 1) // 2
    steps_a, steps_b = tuple(range(first_count)), tuple(range(first_count, step_count))
    shape = (step_count, half, rhs)
    units = far_units((steps_a, steps_b))
    together = lax.optimization_barrier

    def scatter(send, keep, after):
        pieces = split(split_at, keep, swap(send, "blk", size, 1), len(outward), after)
        return pieces[0], [swap(piece, "blk", size, mask) for mask, piece in zip(outward[1:], pieces[1:])], pieces[1]

    def collect(own, got):
        for piece in got:
            own = own + piece.astype(F32)
        part = own.astype(BF)
        for bit in range(halvings, bits - 1):
            part = (part.astype(F32) + swap(part, "blk", size, 1 << bit).astype(F32)).astype(BF)
        return part, swap(part, "blk", size, 1 << (bits - 1))

    def remain(load, part, got):
        return load - (part.astype(F32) + got.astype(F32)).reshape(load.shape)

    def spread(answer):
        return [swap(answer, "blk", size, mask) for mask in cross[1:]]

    def forward(answer, got):
        pieces = [answer] + got
        return pieces + [swap(piece, "blk", size, 1) for piece in pieces]

    send, keep = gemm(core, panel, solved, steps_a, [])
    sent = pack(units, core, inverses, window, send)
    here = lax.ppermute(sent, "rows", pair)
    own_a, got_a, after = scatter(send, keep, [sent])
    send, keep = gemm(core, panel, solved, steps_b, [after])
    send, got_a = together((send, got_a))
    own_b, got_b, after = scatter(send, keep, [])
    load_a, load_b = cut(mine.astype(jnp.int32)[None], loads, cols, (len(steps_a), len(steps_b)), after)
    part_a, half_a = collect(own_a, got_a)
    here = anchor(here, [after])
    half_a = anchor(half_a, [load_a])
    tiles_b = fetch(window, steps_b, block, load_a)
    got_b[-1] = anchor(got_b[-1], [half_a, tiles_b])
    part_b, half_b = collect(own_b, got_b)
    left_a = remain(load_a, part_a, half_a)
    far_a = lax.ppermute(left_a.astype(BF), "rows", pair)
    there = swap(here, "blk", size, 1)
    far_w = unpack(core, here, there)
    answer_a, load_b = chain(units, steps_a, side, inverses, far_w, left_a, far_a, [window, load_b], [])
    got_a = spread(answer_a)
    left_b = remain(load_b, part_b, anchor(half_b, [load_b]))
    rounded = left_b.astype(BF)
    far_b = lax.ppermute(rounded, "rows", pair)
    (answer_b,) = chain(units, steps_b, side, inverses, far_w, left_b, far_b, [tiles_b], got_a)
    got_b = spread(answer_b)
    pieces = [(steps_a[0], put_at[i], piece) for i, piece in enumerate(forward(answer_a, got_a))]
    pieces += [(steps_b[0], put_at[i], piece) for i, piece in enumerate(forward(answer_b, got_b))]
    return put(shape, pieces)


def solution(mesh):
    placed = (
        P(None, "rows", "blk"),
        P("blk", None),
        P(None, "rows", None),
        P(None, "rows", None),
        P(None, "rows", None),
    )
    return jax.shard_map(
        functools.partial(shards, mesh.shape["blk"]),
        mesh=mesh,
        in_specs=placed,
        out_specs=P(None, "rows", None),
        check_vma=False,
    )
```
